768 devices in a mesh: aux: 12 (over z), orb: 64 (over y, x, core).
Axes of the slice: x: 4, y: 8, z: 12, core: 2. Of those that a mesh axis runs over, the one named last changes fastest.
Arguments:
- three_centre: bfloat16 [768, 128, 4096], P('aux', 'orb'), may hold values from -0.75 to 0.75
- occ_table: bfloat16 [3072, 4096], P(('aux', 'orb')), may hold values from -0.75 to 0.75
- vir_table: bfloat16 [3072, 4096], P(('aux', 'orb')), may hold values from -0.75 to 0.75
- term_blocks: int32 [12, 2048, 2], P('aux', 'orb'), may hold values from 0 to 1
- green_ids: int32 [12, 2048, 2], P('aux', 'orb'), may hold values from 0 to 3071, as said below
- live_terms: int32 [12, 64], P('aux', 'orb'), may hold values from 1 to 32, 1536 in all within a row
Outputs:
- response: float32 [768, 64], P(('aux', 'orb'))
The draws below stay inside these ranges and needn't reach their ends.
Inputs may be any that keep to these rules, and one draw needn't show every extreme that they name: `green_ids`: block g of either Green's table is held by orb index (g // 4) % 64. In each of the two columns, the 32 ids of one device, counted with repeats, fall on the blocks of any one orb index at most 2 times.
All inputs are finite; a program needn't handle non-finite values. No bound on the sum of `live_terms` on one device may be relied on, other than what follows from the above.
Results may differ from the reference program's by a relative error of at most 0.004.
Values may be sent and summed in bfloat16 or wider, within the bound.
A program may use at most 64 MiB of HBM per device.

```python
import math
import jax
import jax.numpy as jnp
import numpy as np
from jax import lax

BS = 64
PA = 64
KB = 2
NT = 32
CAP = 2
GB_DEV = 4
AUXF = 768
NBLK = 128
TERMS = 2048
NG = 3072
N_AUX = 12
N_ORB = 64


def draw_green_ids(key, part):
    key = jax.random.fold_in(key, 7)

    def one_table(table_key):
        popular = jax.random.randint(jax.random.fold_in(table_key, 1), (), 0, N_ORB)
        others = jnp.arange(N_ORB - 1, dtype=jnp.int32)
        others = jnp.where(others >= popular, others + 1, others)
        owner_pool = jnp.repeat(others, CAP)
        device_keys = jax.random.split(jax.random.fold_in(table_key, 2), N_AUX * N_ORB)

        def one_device(device_key):
            key_pool, key_order, key_rows = jax.random.split(device_key, 3)
            shuffle = jax.random.permutation(key_pool, owner_pool.shape[0])
            rest = owner_pool[shuffle[:NT - CAP]]
            owners = jnp.concatenate([jnp.full((CAP,), popular, jnp.int32), rest])
            owners = owners[jax.random.permutation(key_order, NT)]
            local_rows = jax.random.randint(key_rows, (NT,), 0, GB_DEV * N_AUX)
            return (local_rows // GB_DEV * N_ORB + owners) * GB_DEV + local_rows % GB_DEV
        return jax.vmap(one_device)(device_keys)
    first_table = one_table(jax.random.fold_in(key, 1))
    second_table = one_table(jax.random.fold_in(key, 2))
    stacked = jnp.stack([first_table, second_table], axis=-1)
    return stacked.reshape(N_AUX, N_ORB * NT, 2).astype(jnp.int32)


def touch_ends(array, stream_key, smallest, largest):
    extent = array.shape
    spot = [jax.random.randint(jax.random.fold_in(stream_key, axis), (), 0, extent[axis]) for axis in range(len(extent))]
    array = array.at[tuple(spot)].set(smallest)
    longest = extent.index(max(extent))
    spot[longest] = (spot[longest] + 1) % extent[longest]
    return array.at[tuple(spot)].set(largest)


def with_spikes(entries, key, source, target, shards_of, factor):
    owner, partner = [(jnp.arange(entries.shape[dim]) // (entries.shape[dim] // shards_of)).reshape([-1 if axis == dim else 1 for axis in range(entries.ndim)]) for dim in (source, target)]
    chosen = jax.random.permutation(key, shards_of)[partner]
    strong = (owner == chosen) | (owner == (partner + shards_of // 2) % shards_of)
    return jnp.where(strong, factor * entries, entries)


def shard_levels(stream_key, shape, pieces, low, largest):
    level = 1.0
    for dim, shards_of in pieces:
        steps = jax.random.uniform(jax.random.fold_in(jax.random.fold_in(stream_key, 6), dim), (shards_of,), jnp.float32, low / len(pieces), largest / len(pieces))
        level = level * jnp.repeat(jnp.exp(steps), shape[dim] // shards_of).reshape((-1,) + (1,) * (len(shape) - 1 - dim))
    return level


def profile(count, total, reach, slope):
    loads = [(1 << 20) // math.isqrt(rank ** slope) + 1 for rank in range(2, count + 1)]
    surplus, holding = total - reach - (count - 1), [1] * (count - 1)
    while surplus > 0:
        free = [i for i in range(count - 1) if holding[i] < reach]
        whole, left = sum([loads[i] for i in free]), surplus
        for i in free:
            addition = min(reach - holding[i], max(1, left * loads[i] // whole), surplus)
            holding[i] = holding[i] + addition
            surplus = surplus - addition
    return np.array([reach] + holding)


def uneven(rng, count, total, most, skew):
    if count == 2:
        one = jax.random.randint(rng, (), max(1, total - most), min(most, total - 1) + 1)
        return jnp.stack([one, total - one])
    tallies = jnp.asarray(profile(count, total, most, skew), jnp.int32)
    twos = (count - 1) // 2
    donor, receiver = tallies[1:1 + 2 * twos:2], tallies[2:2 + 2 * twos:2]
    margin = jnp.minimum(donor - 1, most - receiver)
    passed = jax.random.randint(jax.random.fold_in(rng, 1), (twos,), 0, 1 << 20) % (margin + 1)
    tallies = tallies.at[1:1 + 2 * twos:2].set(donor - passed).at[2:2 + 2 * twos:2].set(receiver + passed)
    return tallies[jax.random.permutation(jax.random.fold_in(rng, 2), count)]


def scatter_about(stream_key, dims, spread, reach, pieces=(), kind=jnp.bfloat16):
    array = jax.random.normal(stream_key, dims, jnp.float32) * spread
    if len(pieces) > 0:
        array = shard_levels(stream_key, dims, pieces, -0.22, 0.18) * array
    return jnp.clip(array, min=-reach, max=reach).astype(kind)


def gaussian_with(stream_key, dims, scale, reach, shards, heavy, held_as=jnp.bfloat16):
    drawn = scale * jax.random.normal(stream_key, dims, jnp.float32)
    if shards:
        drawn = drawn * shard_levels(stream_key, dims, shards, -0.22, 0.18)
    return jnp.clip(with_spikes(drawn, jax.random.fold_in(stream_key, 3), *heavy), -reach, reach).astype(held_as)


def setup_inputs(seed: int = 0) -> dict:
    key_list = jax.random.split(jax.random.key(seed), 7)
    return {
        "three_centre": gaussian_with(key_list[0], (AUXF, NBLK, BS * BS), ((BS * BS * NT * N_ORB) ** -0.25), 0.75, ((0, 12), (1, 64)), (1, 0, 64, 4.0)),
        "occ_table": scatter_about(key_list[1], (NG, BS * BS), BS ** -0.5, 0.75, ((0, 768),)),
        "vir_table": scatter_about(key_list[2], (NG, BS * BS), BS ** -0.5, 0.75, ((0, 768),)),
        "term_blocks": touch_ends(jax.random.randint(key_list[3], (N_AUX, TERMS, 2), 0, KB), jax.random.fold_in(key_list[3], 1), 0, KB - 1).astype(jnp.int32),
        "green_ids": draw_green_ids(jax.random.fold_in(key_list[6], 71), 0),
        "live_terms": jax.vmap(lambda own: uneven(own, N_ORB, (3 * NT * N_ORB) // 4, NT, 1))(jax.random.split(key_list[5], N_AUX)).reshape((N_AUX, N_ORB)).astype(jnp.int32),
    }


def device_response(b_dev, block_pairs, green_rows, live_count, occ_table, vir_table):
    def add_term(running, position):
        first_block = jnp.take(b_dev, block_pairs[position, 0], axis=1).reshape(PA, BS, BS)
        partner = jnp.take(b_dev, block_pairs[position, 1], axis=1)
        density = occ_table[green_rows[position, 0]].reshape(BS, BS)
        virtual = vir_table[green_rows[position, 1]].reshape(BS, BS)
        half = jnp.einsum("pml,mn->pnl", first_block.astype(jnp.float32), density.astype(jnp.float32)).astype(jnp.bfloat16)
        twice = jnp.einsum("pnl,ls->pns", half.astype(jnp.float32), virtual.astype(jnp.float32)).astype(jnp.bfloat16)
        contribution = jnp.dot(twice.reshape(PA, BS * BS), partner.T, preferred_element_type=jnp.float32)
        weight = (position < live_count).astype(jnp.float32)
        return running + weight * contribution, None

    running, _ = lax.scan(add_term, jnp.zeros((PA, PA), jnp.float32), jnp.arange(NT, dtype=jnp.int32))
    return running


def reference(three_centre, occ_table, vir_table, term_blocks, green_ids, live_terms):
    def slab_response(slab):
        b_slab = lax.dynamic_slice_in_dim(three_centre, slab * PA, PA, 0)

        def over_orb(running, orb_index):
            b_dev = lax.dynamic_slice_in_dim(b_slab, orb_index * KB, KB, 1)
            pairs_dev = lax.dynamic_slice_in_dim(term_blocks[slab], orb_index * NT, NT, 0)
            green_dev = lax.dynamic_slice_in_dim(green_ids[slab], orb_index * NT, NT, 0)
            live_count = live_terms[slab, orb_index]
            return running + device_response(b_dev, pairs_dev, green_dev, live_count, occ_table, vir_table), None

        running, _ = lax.scan(over_orb, jnp.zeros((PA, PA), jnp.float32), jnp.arange(N_ORB, dtype=jnp.int32))
        return running

    slabs = lax.map(slab_response, jnp.arange(N_AUX, dtype=jnp.int32))
    return slabs.reshape(N_AUX * PA, PA)
```

```python
import functools

import jax
import jax.numpy as jnp
from jax import lax
from jax.experimental import pallas as pl
from jax.experimental.pallas import tpu as pltpu
from jax.sharding import PartitionSpec as P

BS = 64
NT = 32
GB_DEV = 4
ROWS = 8
COLS = 8
NZ = 12
REACH = 2
PEERS = (2 * REACH + 1) * COLS
MESH = pl.DeviceIdType.MESH
BF = jnp.bfloat16


def wait_bytes(ref, sem):
    pltpu.make_async_copy(ref, ref, sem).wait()


def exchange_kernel(
    slots, occ, vir, requests, dens_out, virt_out,
    held_o, held_v, near_o, near_v, far_o, far_v, got_o, got_v, asked, asked_s,
    req_send, req_recv, copy_sem, swap_send, swap_recv, ring_send, ring_recv,
    out_send, out_recv,
):
    z = lax.axis_index("aux")
    orb = lax.axis_index("orb")
    y, c = orb // COLS, orb % COLS
    half = y // (ROWS // 2)
    pair = (y % (ROWS // 2)) * COLS + c
    right, left = lax.rem(z + 1, NZ), lax.rem(z + NZ - 1, NZ)
    opposite = lax.rem(y + ROWS // 2, ROWS) * COLS + c

    def peer(e, j):
        return lax.rem(y + e + ROWS, ROWS) * COLS + lax.rem(c + j, COLS)

    barrier = pltpu.get_barrier_semaphore()
    pl.semaphore_signal(barrier, inc=1, device_id=(right, orb), device_id_type=MESH)
    pl.semaphore_signal(barrier, inc=1, device_id=(left, orb), device_id_type=MESH)
    pl.semaphore_signal(barrier, inc=1, device_id=(z, opposite), device_id_type=MESH)

    def greet(i, _):
        pl.semaphore_signal(
            barrier, inc=1, device_id=(z, peer(i // COLS - REACH, i % COLS)), device_id_type=MESH
        )
        return _

    middle = REACH * COLS
    lax.fori_loop(0, middle, greet, 0)
    lax.fori_loop(middle + 1, PEERS, greet, 0)
    pl.semaphore_wait(barrier, PEERS + 2)

    held = (held_o, held_v)
    own = (occ, vir)

    def chunk(t, h, origin):
        return held[t].at[pl.ds((h * NZ + origin) * GB_DEV, GB_DEV)]

    swaps = []
    for t in range(2):
        swap = pltpu.make_async_remote_copy(
            src_ref=own[t], dst_ref=chunk(t, half, z), send_sem=swap_send.at[t], recv_sem=swap_recv.at[t],
            device_id=(z, opposite), device_id_type=MESH,
        )
        swap.start()
        swaps.append(swap)
    keeps = []
    for t in range(2):
        keep = pltpu.make_async_copy(own[t], chunk(t, half, z), copy_sem.at[t])
        keep.start()
        keeps.append(keep)

    def ask(i, _):
        e, j = i // COLS - REACH, i % COLS
        pltpu.make_async_remote_copy(
            src_ref=requests, dst_ref=asked.at[(REACH - e) * COLS + c], send_sem=req_send, recv_sem=req_recv,
            device_id=(z, peer(e, j)), device_id_type=MESH,
        ).start()
        return _

    def hop(t, other, way, step):
        h = (1 - half) if other else half
        origin = lax.rem(z - (step - 1) + NZ, NZ) if way == 0 else lax.rem(z + step - 1, NZ)
        src = own[t] if (step == 1 and not other) else chunk(t, h, origin)
        k = 2 * t + other
        return pltpu.make_async_remote_copy(
            src_ref=src, dst_ref=chunk(t, h, origin),
            send_sem=ring_send.at[k, way, step - 1], recv_sem=ring_recv.at[k, way, step - 1],
            device_id=(right if way == 0 else left, orb), device_id_type=MESH,
        )

    steps = (NZ // 2, NZ // 2 - 1)
    lags = {(0, 0): 0, (0, 1): 2, (1, 0): 4, (1, 1): 6}
    events = []
    for (t, other), lag in lags.items():
        for step in range(1, steps[0] + 2):
            events.append((step + lag, t, other, step))
    events.sort()

    def run(event):
        _, t, other, step = event
        for way in range(2):
            if step - 1 >= 1 and step - 1 <= steps[way]:
                hop(t, other, way, step - 1).wait_recv()
        if step == 1 and other:
            swaps[t].wait_recv()
        for way in range(2):
            if step <= steps[way]:
                hop(t, other, way, step).start()

    near, far, got = (near_o, near_v), (far_o, far_v), (got_o, got_v)

    def send_table(t):
        def serve_near(i, _):
            e, j = i // COLS - 1, i % COLS
            d = peer(e, j)
            place = (e + REACH) * COLS + d % COLS
            for col in range(2):
                for rank in range(2):
                    row = asked_s[place, t, pair * 4 + col * 2 + rank]
                    near[t][i, col * 2 + rank] = held[t][col * NZ * GB_DEV + row]
            return d

        def near_remote(i, _):
            d = serve_near(i, _)
            pltpu.make_async_remote_copy(
                src_ref=near[t].at[i], dst_ref=got[t].at[pair], send_sem=out_send.at[t], recv_sem=out_recv.at[t],
                device_id=(z, d), device_id_type=MESH,
            ).start()
            return _

        def far_remote(i, _):
            e, j = (i // COLS) * 2 * REACH - REACH, i % COLS
            d = peer(e, j)
            place = (e + REACH) * COLS + d % COLS
            for rank in range(2):
                row = asked_s[place, t, pair * 4 + half * 2 + rank]
                far[t][i, rank] = held[t][half * NZ * GB_DEV + row]
            pltpu.make_async_remote_copy(
                src_ref=far[t].at[i], dst_ref=got[t].at[pair, pl.ds(half * 2, 2)],
                send_sem=out_send.at[t], recv_sem=out_recv.at[t],
                device_id=(z, d), device_id_type=MESH,
            ).start()
            return _

        lax.fori_loop(0, 2 * COLS, far_remote, 0)
        lax.fori_loop(0, COLS, near_remote, 0)
        lax.fori_loop(2 * COLS, 3 * COLS, near_remote, 0)
        lax.fori_loop(COLS + 1, 2 * COLS, near_remote, 0)
        serve_near(COLS, 0)
        pltpu.make_async_copy(near[t].at[COLS], got[t].at[pair], out_recv.at[t]).start()

    last_o = max(i for i, ev in enumerate(events) if ev[1] == 0)
    for i, event in enumerate(events):
        run(event)
        if i == 1:
            lax.fori_loop(0, middle, ask, 0)
            lax.fori_loop(middle + 1, PEERS, ask, 0)
            mine = pltpu.make_async_copy(requests, asked.at[middle + c], req_recv)
            mine.start()
        if i == last_o:
            keeps[0].wait()
            wait_bytes(asked, req_recv)
            to_smem = pltpu.make_async_copy(asked, asked_s, copy_sem.at[2])
            to_smem.start()
            to_smem.wait()
            send_table(0)
    keeps[1].wait()
    send_table(1)

    wait_bytes(got_o, out_recv.at[0])
    for t in range(NT):
        s = slots[0, t]
        dens_out[t] = got_o[s // 4, s % 4]
    wait_bytes(got_v, out_recv.at[1])
    for t in range(NT):
        s = slots[1, t]
        virt_out[t] = got_v[s // 4, s % 4]

    wait_bytes(asked.at[pl.ds(0, PEERS - 1)], req_send)
    for t in range(2):
        swaps[t].wait_send()
        wait_bytes(near[t].at[pl.ds(0, 3 * COLS - 1)], out_send.at[t])
        wait_bytes(far[t], out_send.at[t])
        for other in range(2):
            for way in range(2):
                for step in range(1, steps[way] + 1):
                    hop(t, other, way, step).wait_send()


def exchange(slots, occ, vir, requests):
    block = (BS // 2, 2 * BS)
    vmem = pl.BlockSpec(memory_space=pltpu.VMEM)
    return pl.pallas_call(
        exchange_kernel,
        out_shape=[jax.ShapeDtypeStruct((NT, *block), BF)] * 2,
        in_specs=[pl.BlockSpec(memory_space=pltpu.SMEM), vmem, vmem, vmem],
        out_specs=[vmem, vmem],
        scratch_shapes=[
            *[pltpu.VMEM((2 * NZ * GB_DEV, *block), BF)] * 2,
            *[pltpu.VMEM((3 * COLS, 4, *block), BF)] * 2,
            *[pltpu.VMEM((2 * COLS, 2, *block), BF)] * 2,
            *[pltpu.VMEM((ROWS // 2 * COLS, 4, *block), BF)] * 2,
            pltpu.VMEM((PEERS, 2, 128), jnp.int32),
            pltpu.SMEM((PEERS, 2, 128), jnp.int32),
            pltpu.SemaphoreType.DMA,
            pltpu.SemaphoreType.DMA,
            pltpu.SemaphoreType.DMA((3,)),
            pltpu.SemaphoreType.DMA((2,)),
            pltpu.SemaphoreType.DMA((2,)),
            pltpu.SemaphoreType.DMA((4, 2, NZ // 2)),
            pltpu.SemaphoreType.DMA((4, 2, NZ // 2)),
            pltpu.SemaphoreType.DMA((2,)),
            pltpu.SemaphoreType.DMA((2,)),
        ],
        compiler_params=pltpu.CompilerParams(
            collective_id=0, has_side_effects=True, vmem_limit_bytes=48 * 2**20
        ),
        name="exchange",
    )(slots, occ, vir, requests)


def spread(packed, lanes):
    wide = packed.astype(jnp.float32)
    turned = pltpu.roll(wide, BS, 1)
    zero = jnp.zeros_like(wide)
    low = lanes < BS
    left = jnp.concatenate([jnp.where(low, wide, zero), jnp.where(low, turned, zero)], axis=0)
    right = jnp.concatenate([jnp.where(low, zero, turned), jnp.where(low, zero, wide)], axis=0)
    return left, right


def math_kernel(pairs, live, dens, virt, x_ref, b_ref, out, a_s, w_s, h_s, s_s, t_s):
    lanes = lax.broadcasted_iota(jnp.int32, (BS // 2, 2 * BS), 1)

    def build(t, _):
        first, second = pairs[0, t], pairs[1, t]
        alive = (t < live[0]).astype(jnp.float32)
        left, right = spread(dens[t], lanes)
        at = pl.multiple_of(t * BS, BS)
        a_s[pl.ds(at, BS), :] = (jnp.where(first == 0, left, right) * alive).astype(BF)
        left, right = spread(virt[t], lanes)
        at = pl.multiple_of(t * 2 * BS, 2 * BS)
        for k in range(2):
            on = (second == k).astype(jnp.float32)
            w_s[pl.ds(at, BS), k * 128:(k + 1) * 128] = (left * on).astype(BF)
            w_s[pl.ds(at + BS, BS), k * 128:(k + 1) * 128] = (right * on).astype(BF)
        return _

    lax.fori_loop(0, NT, build, 0)

    group = 8

    def first_product(j, _):
        weights = x_ref[j]
        at = pl.multiple_of(j * 128, 128)
        for g in range(NT // group):
            part = jnp.dot(
                a_s[g * group * BS:(g + 1) * group * BS, :], weights, preferred_element_type=jnp.float32
            ).astype(BF)
            for i in range(group):
                t = g * group + i
                for k in range(2):
                    h_s[pl.ds(at + k * BS, BS), t * 128:(t + 1) * 128] = part[
                        i * BS:(i + 1) * BS, k * 128:(k + 1) * 128
                    ]
        return _

    lax.fori_loop(0, 16, first_product, 0)

    rows = 256

    def second_product(j, _):
        at = pl.multiple_of(j * rows, rows)
        total = jnp.dot(h_s[pl.ds(at, rows), :], w_s[...], preferred_element_type=jnp.float32)
        for k in range(2):
            s_s[k, pl.ds(at, rows), :] = total[:, k * 128:(k + 1) * 128]
        return _

    lax.fori_loop(0, 2048 // rows, second_product, 0)

    low = lanes < BS
    for n in range(0, BS, 2):
        for k in range(2):
            even = s_s[k, pl.ds(n, 32, stride=BS), :]
            odd = s_s[k, pl.ds(n + 1, 32, stride=BS), :]
            at = k * BS * BS + n * BS
            t_s[0:32, at:at + 128] = jnp.where(low, even, pltpu.roll(odd, BS, 1)).astype(BF)
            t_s[32:64, at:at + 128] = jnp.where(low, pltpu.roll(even, BS, 1), odd).astype(BF)
    out[...] = lax.dot_general(
        t_s[...], b_ref[...], (((1,), (1,)), ((), ())), preferred_element_type=jnp.float32
    )


def math(pairs, live, dens, virt, x, b):
    vmem = pl.BlockSpec(memory_space=pltpu.VMEM)
    smem = pl.BlockSpec(memory_space=pltpu.SMEM)
    return pl.pallas_call(
        math_kernel,
        out_shape=jax.ShapeDtypeStruct((BS, BS), jnp.float32),
        in_specs=[smem, smem, vmem, vmem, vmem, vmem],
        out_specs=vmem,
        scratch_shapes=[
            pltpu.VMEM((NT * BS, 128), BF),
            pltpu.VMEM((NT * 128, 256), BF),
            pltpu.VMEM((2048, NT * 128), BF),
            pltpu.VMEM((2, 2048, 128), jnp.float32),
            pltpu.VMEM((BS, 2 * BS * BS), BF),
        ],
        compiler_params=pltpu.CompilerParams(vmem_limit_bytes=56 * 2**20),
        name="math",
    )(pairs, live, dens, virt, x, b)


def rows_kernel(r_ref, out, got, send, recv):
    z = lax.axis_index("aux")
    me = lax.axis_index("orb")
    count = ROWS * COLS
    barrier = pltpu.get_barrier_semaphore()

    def greet(i, _):
        pl.semaphore_signal(barrier, inc=1, device_id=(z, lax.rem(me + i, count)), device_id_type=MESH)
        return _

    lax.fori_loop(1, count, greet, 0)
    pl.semaphore_wait(barrier, count - 1)

    def give(i, _):
        to = lax.rem(me + i, count)
        pltpu.make_async_remote_copy(
            src_ref=r_ref.at[to], dst_ref=got.at[me], send_sem=send, recv_sem=recv,
            device_id=(z, to), device_id_type=MESH,
        ).start()
        return _

    lax.fori_loop(1, count, give, 0)
    pltpu.make_async_copy(r_ref.at[me], got.at[me], recv).start()
    wait_bytes(got, recv)
    out[...] = jnp.sum(got[...], axis=0)
    wait_bytes(got.at[pl.ds(0, count - 1)], send)


def add_rows(r):
    vmem = pl.BlockSpec(memory_space=pltpu.VMEM)
    return pl.pallas_call(
        rows_kernel,
        out_shape=jax.ShapeDtypeStruct((1, BS), jnp.float32),
        in_specs=[vmem],
        out_specs=vmem,
        scratch_shapes=[
            pltpu.VMEM((ROWS * COLS, 1, BS), jnp.float32),
            pltpu.SemaphoreType.DMA,
            pltpu.SemaphoreType.DMA,
        ],
        compiler_params=pltpu.CompilerParams(collective_id=1, has_side_effects=True),
        name="add_rows",
    )(r)


def local(three_centre, occ_table, vir_table, term_blocks, green_ids, live_terms):
    orb_count = ROWS * COLS
    green = green_ids[0]
    group = green // GB_DEV
    owner = group % orb_count
    row = group // orb_count * GB_DEV + green % GB_DEV
    position = jnp.arange(NT, dtype=jnp.int32)
    earlier = position[:, None] > position[None, :]
    same = owner[:, None, :] == owner[None, :, :]
    rank = jnp.sum(jnp.logical_and(same, earlier[:, :, None]).astype(jnp.int32), axis=1)
    y, c = owner // COLS, owner % COLS
    slots = ((y % 4) * COLS + c) * 4 + (y // 4) * 2 + rank
    match = slots[:, :, None] == jnp.arange(128, dtype=jnp.int32)[None, None, :]
    requests = jnp.sum(jnp.where(match, row[:, :, None], 0), axis=0)

    occ = occ_table.reshape(GB_DEV, BS, 2, 32).transpose(0, 3, 2, 1).reshape(GB_DEV, 32, 128)
    vir = vir_table.reshape(GB_DEV, 2, 32, BS).transpose(0, 2, 1, 3).reshape(GB_DEV, 32, 128)
    dens, virt = exchange(slots.T, occ, vir, requests)

    x = three_centre.reshape(2, 16, 2, 2, BS, BS).transpose(1, 3, 4, 2, 0, 5).reshape(16, 128, 256)
    b = three_centre.reshape(BS, 2 * BS * BS)
    r = math(term_blocks[0].T, live_terms.reshape(1), dens, virt, x, b)
    return add_rows(r.reshape(BS, 1, BS))


def solution(mesh):
    return jax.shard_map(
        local,
        mesh=mesh,
        in_specs=(
            P("aux", "orb", None),
            P(("aux", "orb"), None),
            P(("aux", "orb"), None),
            P("aux", "orb", None),
            P("aux", "orb", None),
            P("aux", "orb"),
        ),
        out_specs=P(("aux", "orb"), None),
        check_vma=False,
    )
```

```python
import functools

import jax
import jax.numpy as jnp
from jax import lax
from jax.experimental import pallas as pl
from jax.experimental.pallas import tpu as pltpu
from jax.sharding import PartitionSpec as P

BS = 64
NT = 32
GB_DEV = 4
ROWS = 8
COLS = 8
NZ = 12
REACH = 2
PEERS = (2 * REACH + 1) * COLS
ORBS = ROWS * COLS
MESH = pl.DeviceIdType.MESH
BF = jnp.bfloat16


def wait_bytes(ref, sem):
    pltpu.make_async_copy(ref, ref, sem).wait()


def spread(packed, lanes):
    wide = packed.astype(jnp.float32)
    turned = pltpu.roll(wide, BS, 1)
    zero = jnp.zeros_like(wide)
    low = lanes < BS
    left = jnp.concatenate([jnp.where(low, wide, zero), jnp.where(low, turned, zero)], axis=0)
    right = jnp.concatenate([jnp.where(low, zero, turned), jnp.where(low, zero, wide)], axis=0)
    return left, right


def kernel(
    slots, pairs, live, occ, vir, requests, b_ref, out,
    held_o, held_v, twin_o, twin_v, own_o, own_v, other_o, other_v, got_o, got_v, asked, asked_s,
    x_s, a_s, w_s, h_s, s_s, t_s, r_s, row_s, rows_got,
    req_send, req_recv, copy_sem, swap_send, swap_recv, ring_send, ring_recv,
    out_send, out_recv, row_send, row_recv,
):
    z = lax.axis_index("aux")
    orb = lax.axis_index("orb")
    y, c = orb // COLS, orb % COLS
    half = y // (ROWS // 2)
    pair = (y % (ROWS // 2)) * COLS + c
    right, left = lax.rem(z + 1, NZ), lax.rem(z + NZ - 1, NZ)
    opposite = lax.rem(y + ROWS // 2, ROWS) * COLS + c
    lanes = lax.broadcasted_iota(jnp.int32, (BS // 2, 2 * BS), 1)
    low = lanes < BS

    def peer(e, j):
        return lax.rem(y + e + ROWS, ROWS) * COLS + lax.rem(c + j, COLS)

    barrier = pltpu.get_barrier_semaphore()
    pl.semaphore_signal(barrier, inc=1, device_id=(right, orb), device_id_type=MESH)
    pl.semaphore_signal(barrier, inc=1, device_id=(left, orb), device_id_type=MESH)

    def greet(i, _):
        pl.semaphore_signal(barrier, inc=1, device_id=(z, lax.rem(orb + i, ORBS)), device_id_type=MESH)
        return _

    lax.fori_loop(1, ORBS, greet, 0)

    for k in range(2):
        for m in range(0, BS, 2):
            at = (k * BS + m) * BS
            upper = b_ref[0:32, at:at + 128].astype(jnp.float32)
            lower = b_ref[32:64, at:at + 128].astype(jnp.float32)
            row = k * BS + m
            x_s[pl.ds(row, 32, stride=128), :] = jnp.where(low, upper, pltpu.roll(lower, BS, 1))
            x_s[pl.ds(row + 1, 32, stride=128), :] = jnp.where(low, pltpu.roll(upper, BS, 1), lower)

    pl.semaphore_wait(barrier, ORBS + 1)

    held = ((held_o, twin_o), (held_v, twin_v))
    own = (occ, vir)

    def chunk(t, other, origin):
        return held[t][other].at[pl.ds(origin * GB_DEV, GB_DEV)]

    def hop(t, other, way, step):
        origin = lax.rem(z - (step - 1) + NZ, NZ) if way == 0 else lax.rem(z + step - 1, NZ)
        src = own[t] if (step == 1 and not other) else chunk(t, other, origin)
        k = 2 * t + other
        return pltpu.make_async_remote_copy(
            src_ref=src, dst_ref=chunk(t, other, origin),
            send_sem=ring_send.at[k, way, step - 1], recv_sem=ring_recv.at[k, way, step - 1],
            device_id=(right if way == 0 else left, orb), device_id_type=MESH,
        )

    swaps = [
        pltpu.make_async_remote_copy(
            src_ref=own[t], dst_ref=chunk(t, 1, z), send_sem=swap_send.at[t], recv_sem=swap_recv.at[t],
            device_id=(z, opposite), device_id_type=MESH,
        )
        for t in range(2)
    ]
    keeps = [pltpu.make_async_copy(own[t], chunk(t, 0, z), copy_sem.at[t]) for t in range(2)]
    steps = (NZ // 2, NZ // 2 - 1)

    def run(t, other, step):
        for way in range(2):
            if 1 <= step - 1 <= steps[way]:
                hop(t, other, way, step - 1).wait_recv()
        if step == 1 and other:
            swaps[t].wait_recv()
        for way in range(2):
            if step <= steps[way]:
                hop(t, other, way, step).start()

    def ask(e, j):
        pltpu.make_async_remote_copy(
            src_ref=requests, dst_ref=asked.at[(REACH - e) * COLS + c], send_sem=req_send, recv_sem=req_recv,
            device_id=(z, peer(e, j)), device_id_type=MESH,
        ).start()

    def ask_row(i, _):
        for j in range(COLS):
            ask(i - REACH + i // REACH, j)
        return _

    outs, got = ((own_o, other_o), (own_v, other_v)), (got_o, got_v)

    def serve(t, other, e, j, remote):
        d = peer(e, j)
        h = (1 - half) if other else half
        place = (e + REACH) * COLS + d % COLS
        slot = ((e + 1) if other else (e + REACH)) * COLS + j
        box = outs[t][other]
        for rank in range(2):
            row = asked_s[place, t, pair * 4 + h * 2 + rank]
            box[slot, rank] = held[t][other][row]
        to = got[t].at[pair, pl.ds(h * 2, 2)]
        if remote:
            pltpu.make_async_remote_copy(
                src_ref=box.at[slot], dst_ref=to, send_sem=out_send.at[t], recv_sem=out_recv.at[t],
                device_id=(z, d), device_id_type=MESH,
            ).start()
        else:
            pltpu.make_async_copy(box.at[slot], to, out_recv.at[t]).start()

    def send_table(t, other):
        def one_row(i, _):
            e = 2 * i - 1 if other else i - REACH + i // REACH
            for j in range(COLS):
                serve(t, other, e, j, True)
            return _

        lax.fori_loop(0, 2 if other else 2 * REACH, one_row, 0)
        for j in range(1, COLS):
            serve(t, other, 0, j, True)
        serve(t, other, 0, 0, False)

    for t in range(2):
        run(t, 0, 1)
    for t in range(2):
        swaps[t].start()
        keeps[t].start()
    lax.fori_loop(0, 2 * REACH, ask_row, 0)
    for j in range(1, COLS):
        ask(0, j)
    pltpu.make_async_copy(requests, asked.at[REACH * COLS + c], req_recv).start()

    lag = 2
    last = steps[0] + 1
    to_smem = pltpu.make_async_copy(asked, asked_s, copy_sem.at[2])
    for tick in range(2, last + lag + 1):
        for other in range(2):
            step = tick - lag * other
            for t in range(2):
                if 1 <= step <= last:
                    run(t, other, step)
        if tick == 4:
            wait_bytes(asked, req_recv)
            to_smem.start()
        if tick == last:
            to_smem.wait()
            keeps[0].wait()
            send_table(0, 0)
    send_table(0, 1)
    keeps[1].wait()
    send_table(1, 0)
    send_table(1, 1)

    wait_bytes(got_o, out_recv.at[0])

    def build_a(t, _):
        s, first = slots[0, t], pairs[0, t]
        alive = (t < live[0]).astype(jnp.float32)
        on_left, on_right = spread(got_o[s // 4, s % 4], lanes)
        at = pl.multiple_of(t * BS, BS)
        a_s[pl.ds(at, BS), :] = (jnp.where(first == 0, on_left, on_right) * alive).astype(BF)
        return _

    lax.fori_loop(0, NT, build_a, 0)
    group = 8

    def first_product(j, _):
        at = pl.multiple_of(j * 256, 256)
        weights = jnp.concatenate(
            [x_s[pl.ds(at, 128), :].astype(BF), x_s[pl.ds(at + 128, 128), :].astype(BF)], axis=1
        )
        to = pl.multiple_of(j * 128, 128)
        for g in range(NT // group):
            part = jnp.dot(
                a_s[g * group * BS:(g + 1) * group * BS, :], weights, preferred_element_type=jnp.float32
            ).astype(BF)
            for i in range(group):
                t = g * group + i
                for k in range(2):
                    h_s[pl.ds(to + k * BS, BS), t * 128:(t + 1) * 128] = part[
                        i * BS:(i + 1) * BS, k * 128:(k + 1) * 128
                    ]
        return _

    lax.fori_loop(0, 16, first_product, 0)

    wait_bytes(got_v, out_recv.at[1])

    def build_w(t, _):
        s, second = slots[1, t], pairs[1, t]
        on_left, on_right = spread(got_v[s // 4, s % 4], lanes)
        at = pl.multiple_of(t * 2 * BS, 2 * BS)
        for k in range(2):
            on = (second == k).astype(jnp.float32)
            w_s[pl.ds(at, BS), k * 128:(k + 1) * 128] = (on_left * on).astype(BF)
            w_s[pl.ds(at + BS, BS), k * 128:(k + 1) * 128] = (on_right * on).astype(BF)
        return _

    lax.fori_loop(0, NT, build_w, 0)
    rows = 256

    def second_product(j, _):
        at = pl.multiple_of(j * rows, rows)
        total = jnp.dot(h_s[pl.ds(at, rows), :], w_s[...], preferred_element_type=jnp.float32)
        for k in range(2):
            s_s[k, pl.ds(at, rows), :] = total[:, k * 128:(k + 1) * 128]
        return _

    lax.fori_loop(0, 2048 // rows, second_product, 0)

    for n in range(0, BS, 2):
        for k in range(2):
            even = s_s[k, pl.ds(n, 32, stride=BS), :]
            odd = s_s[k, pl.ds(n + 1, 32, stride=BS), :]
            at = k * BS * BS + n * BS
            t_s[0:32, at:at + 128] = jnp.where(low, even, pltpu.roll(odd, BS, 1)).astype(BF)
            t_s[32:64, at:at + 128] = jnp.where(low, pltpu.roll(even, BS, 1), odd).astype(BF)
    r_s[...] = lax.dot_general(
        t_s[...], b_ref[...], (((1,), (1,)), ((), ())), preferred_element_type=jnp.float32
    )
    for i in range(BS):
        row_s[i] = r_s[pl.ds(i, 1), :]

    def give(i, _):
        to = lax.rem(orb + i, ORBS)
        pltpu.make_async_remote_copy(
            src_ref=row_s.at[to], dst_ref=rows_got.at[orb], send_sem=row_send, recv_sem=row_recv,
            device_id=(z, to), device_id_type=MESH,
        ).start()
        return _

    lax.fori_loop(1, ORBS, give, 0)
    pltpu.make_async_copy(row_s.at[orb], rows_got.at[orb], row_recv).start()

    wait_bytes(asked.at[pl.ds(0, PEERS - 1)], req_send)
    for t in range(2):
        swaps[t].wait_send()
        wait_bytes(own_o.at[pl.ds(0, PEERS - 1)], out_send.at[t])
        wait_bytes(other_o.at[pl.ds(0, 3 * COLS - 1)], out_send.at[t])
        for other in range(2):
            for way in range(2):
                for step in range(1, steps[way] + 1):
                    hop(t, other, way, step).wait_send()

    wait_bytes(rows_got, row_recv)
    out[...] = jnp.sum(rows_got[...], axis=0)
    wait_bytes(rows_got.at[pl.ds(0, ORBS - 1)], row_send)


def respond(slots, pairs, live, occ, vir, requests, b):
    block = (BS // 2, 2 * BS)
    vmem = pl.BlockSpec(memory_space=pltpu.VMEM)
    smem = pl.BlockSpec(memory_space=pltpu.SMEM)
    return pl.pallas_call(
        kernel,
        out_shape=jax.ShapeDtypeStruct((1, BS), jnp.float32),
        in_specs=[smem, smem, smem, vmem, vmem, vmem, vmem],
        out_specs=vmem,
        scratch_shapes=[
            *[pltpu.VMEM((NZ * GB_DEV, *block), BF)] * 4,
            *[pltpu.VMEM((PEERS, 2, *block), BF)] * 2,
            *[pltpu.VMEM((3 * COLS, 2, *block), BF)] * 2,
            *[pltpu.VMEM((ROWS // 2 * COLS, 4, *block), BF)] * 2,
            pltpu.VMEM((PEERS, 2, 128), jnp.int32),
            pltpu.SMEM((PEERS, 2, 128), jnp.int32),
            pltpu.VMEM((32 * 128, 128), jnp.float32),
            pltpu.VMEM((NT * BS, 128), BF),
            pltpu.VMEM((NT * 128, 256), BF),
            pltpu.VMEM((2048, NT * 128), BF),
            pltpu.VMEM((2, 2048, 128), jnp.float32),
            pltpu.VMEM((BS, 2 * BS * BS), BF),
            pltpu.VMEM((BS, BS), jnp.float32),
            pltpu.VMEM((ORBS, 1, BS), jnp.float32),
            pltpu.VMEM((ORBS, 1, BS), jnp.float32),
            pltpu.SemaphoreType.DMA,
            pltpu.SemaphoreType.DMA,
            pltpu.SemaphoreType.DMA((3,)),
            pltpu.SemaphoreType.DMA((2,)),
            pltpu.SemaphoreType.DMA((2,)),
            pltpu.SemaphoreType.DMA((4, 2, NZ // 2)),
            pltpu.SemaphoreType.DMA((4, 2, NZ // 2)),
            pltpu.SemaphoreType.DMA((2,)),
            pltpu.SemaphoreType.DMA((2,)),
            pltpu.SemaphoreType.DMA,
            pltpu.SemaphoreType.DMA,
        ],
        compiler_params=pltpu.CompilerParams(
            collective_id=0, has_side_effects=True, vmem_limit_bytes=56 * 2**20
        ),
        name="respond",
    )(slots, pairs, live, occ, vir, requests, b)


def local(three_centre, occ_table, vir_table, term_blocks, green_ids, live_terms):
    green = green_ids[0]
    group = green // GB_DEV
    owner = group % ORBS
    row = group // ORBS * GB_DEV + green % GB_DEV
    position = jnp.arange(NT, dtype=jnp.int32)
    earlier = position[:, None] > position[None, :]
    same = owner[:, None, :] == owner[None, :, :]
    rank = jnp.sum(jnp.logical_and(same, earlier[:, :, None]).astype(jnp.int32), axis=1)
    y, c = owner // COLS, owner % COLS
    slots = ((y % 4) * COLS + c) * 4 + (y // 4) * 2 + rank
    match = slots[:, :, None] == jnp.arange(128, dtype=jnp.int32)[None, None, :]
    requests = jnp.sum(jnp.where(match, row[:, :, None], 0), axis=0)

    occ = occ_table.reshape(GB_DEV, BS, 2, 32).transpose(0, 3, 2, 1).reshape(GB_DEV, 32, 128)
    vir = vir_table.reshape(GB_DEV, 2, 32, BS).transpose(0, 2, 1, 3).reshape(GB_DEV, 32, 128)
    b = three_centre.reshape(BS, 2 * BS * BS)
    return respond(slots.T, term_blocks[0].T, live_terms.reshape(1), occ, vir, requests, b)


def solution(mesh):
    return jax.shard_map(
        local,
        mesh=mesh,
        in_specs=(
            P("aux", "orb", None),
            P(("aux", "orb"), None),
            P(("aux", "orb"), None),
            P("aux", "orb", None),
            P("aux", "orb", None),
            P("aux", "orb"),
        ),
        out_specs=P(("aux", "orb"), None),
        check_vma=False,
    )
```

```python
import functools

import jax
import jax.numpy as jnp
from jax import lax
from jax.experimental import pallas as pl
from jax.experimental.pallas import tpu as pltpu
from jax.sharding import PartitionSpec as P

BS = 64
NT = 32
GB_DEV = 4
ROWS = 8
COLS = 8
NZ = 12
REACH = 2
PEERS = (2 * REACH + 1) * COLS
ORBS = ROWS * COLS
MESH = pl.DeviceIdType.MESH
BF = jnp.bfloat16


def wait_bytes(ref, sem):
    pltpu.make_async_copy(ref, ref, sem).wait()


def spread(packed, lanes):
    wide = packed.astype(jnp.float32)
    turned = pltpu.roll(wide, BS, 1)
    zero = jnp.zeros_like(wide)
    low = lanes < BS
    left = jnp.concatenate([jnp.where(low, wide, zero), jnp.where(low, turned, zero)], axis=0)
    right = jnp.concatenate([jnp.where(low, zero, turned), jnp.where(low, zero, wide)], axis=0)
    return left, right


def kernel(
    slots, pairs, live, occ, vir, requests, b_ref, out,
    held, twin, own_o, own_v, other_o, other_v, got_o, got_v, asked, asked_s,
    x_s, a_s, w_s, h_s, s_s, t_s, r_s, row_s, rows_got,
    req_send, req_recv, copy_sem, swap_send, swap_recv, ring_send, ring_recv,
    out_send, out_recv, row_send, row_recv,
):
    z = lax.axis_index("aux")
    orb = lax.axis_index("orb")
    y, c = lax.div(orb, COLS), lax.rem(orb, COLS)
    half = lax.div(y, ROWS // 2)
    pair = lax.rem(y, ROWS // 2) * COLS + c
    right, left = lax.rem(z + 1, NZ), lax.rem(z + NZ - 1, NZ)
    opposite = lax.rem(y + ROWS // 2, ROWS) * COLS + c
    lanes = lax.broadcasted_iota(jnp.int32, (BS // 2, 2 * BS), 1)
    low = lanes < BS

    barrier = pltpu.get_barrier_semaphore()
    pl.semaphore_signal(barrier, inc=1, device_id=(right, orb), device_id_type=MESH)
    pl.semaphore_signal(barrier, inc=1, device_id=(left, orb), device_id_type=MESH)

    def greet(i, _):
        pl.semaphore_signal(barrier, inc=1, device_id=(z, lax.rem(orb + i, ORBS)), device_id_type=MESH)
        return _

    lax.fori_loop(1, ORBS, greet, 0)

    pl.semaphore_wait(barrier, ORBS + 1)

    def lay_out(k):
        for m in range(0, BS, 2):
            at = (k * BS + m) * BS
            upper = b_ref[0:32, at:at + 128].astype(jnp.float32)
            lower = b_ref[32:64, at:at + 128].astype(jnp.float32)
            row = k * BS + m
            x_s[pl.ds(row, 32, stride=128), :] = jnp.where(low, upper, pltpu.roll(lower, BS, 1))
            x_s[pl.ds(row + 1, 32, stride=128), :] = jnp.where(low, pltpu.roll(upper, BS, 1), lower)

    columns = (held, twin)
    outs, got = ((own_o, other_o), (own_v, other_v)), (got_o, got_v)
    own = (occ, vir)
    steps = (NZ // 2, NZ // 2 - 1)

    def hop(other, way, step):
        origin = lax.rem(z - (step - 1) + NZ, NZ) if way == 0 else lax.rem(z + step - 1, NZ)
        return pltpu.make_async_remote_copy(
            src_ref=columns[other].at[origin], dst_ref=columns[other].at[origin],
            send_sem=ring_send.at[other, way, step - 1], recv_sem=ring_recv.at[other, way, step - 1],
            device_id=(right if way == 0 else left, orb), device_id_type=MESH,
        )

    def first_hop(way):
        for t in range(2):
            pltpu.make_async_remote_copy(
                src_ref=own[t], dst_ref=held.at[z, t],
                send_sem=ring_send.at[0, way, 0], recv_sem=ring_recv.at[0, way, 0],
                device_id=(right if way == 0 else left, orb), device_id_type=MESH,
            ).start()

    def run(other, step):
        for way in range(2):
            if 1 <= step - 1 <= steps[way]:
                hop(other, way, step - 1).wait_recv()
            if step <= steps[way]:
                hop(other, way, step).start()

    def peer(e, j):
        return lax.rem(y + e + ROWS, ROWS) * COLS + lax.rem(c + j, COLS)

    def ask(e, j):
        there = lax.rem(y + e + ROWS, ROWS // 2) * COLS + lax.rem(c + j, COLS)
        pltpu.make_async_remote_copy(
            src_ref=requests.at[there], dst_ref=asked.at[(REACH - e) * COLS + c],
            send_sem=req_send, recv_sem=req_recv, device_id=(z, peer(e, j)), device_id_type=MESH,
        ).start()

    def ask_row(i, _):
        for j in range(COLS):
            ask(i - REACH + lax.div(i, REACH), j)
        return _

    def serve(t, other, e, own_row):
        box = outs[t][other]
        slot = (e + (1 if other else REACH)) * COLS
        column = (1 - half) if other else half
        for first in range(0, COLS, 4):
            some = [(j, rank) for j in range(first, first + 4) for rank in range(2)]
            rows = [
                asked_s[(e + REACH) * COLS + lax.rem(c + j, COLS), 0, column * 4 + t * 2 + rank]
                for j, rank in some
            ]
            blocks = [columns[other][lax.div(row, GB_DEV), t, lax.rem(row, GB_DEV)] for row in rows]
            for (j, rank), block in zip(some, blocks):
                box[slot + j, rank] = block
        to = got[t].at[pl.ds(pair * 4 + column * 2, 2)]
        for j in range(COLS):
            if own_row and j == 0:
                pltpu.make_async_copy(box.at[slot], to, out_recv.at[t]).start()
            else:
                pltpu.make_async_remote_copy(
                    src_ref=box.at[slot + j], dst_ref=to, send_sem=out_send.at[t], recv_sem=out_recv.at[t],
                    device_id=(z, peer(e, j)), device_id_type=MESH,
                ).start()

    def send_table(t, other):
        def one_row(i, _):
            serve(t, other, 2 * i - 1 if other else i - REACH + lax.div(i, REACH), False)
            return _

        lax.fori_loop(0, 2 if other else 2 * REACH, one_row, 0)
        serve(t, other, 0, True)

    for way in range(2):
        first_hop(way)
    swaps = [
        pltpu.make_async_remote_copy(
            src_ref=own[t], dst_ref=twin.at[z, t], send_sem=swap_send.at[t], recv_sem=swap_recv.at[t],
            device_id=(z, opposite), device_id_type=MESH,
        )
        for t in range(2)
    ]
    keeps = [pltpu.make_async_copy(own[t], held.at[z, t], copy_sem.at[t]) for t in range(2)]
    for t in range(2):
        swaps[t].start()
        keeps[t].start()
    lax.fori_loop(0, 2 * REACH, ask_row, 0)
    for j in range(1, COLS):
        ask(0, j)
    pltpu.make_async_copy(requests.at[pair], asked.at[REACH * COLS + c], req_recv).start()

    lag = 2
    last = steps[0] + 1
    to_smem = pltpu.make_async_copy(asked, asked_s, copy_sem.at[2])
    for tick in range(2, last + lag + 1):
        if tick <= last:
            run(0, tick)
        if tick == 1 + lag:
            for t in range(2):
                swaps[t].wait_recv()
        if tick > lag:
            run(1, tick - lag)
        if tick in (2, 3):
            lay_out(tick - 2)
        if tick == 5:
            wait_bytes(asked, req_recv)
            to_smem.start()
        if tick == last:
            to_smem.wait()
            for t in range(2):
                keeps[t].wait()
            send_table(0, 0)
    send_table(0, 1)
    send_table(1, 0)
    send_table(1, 1)

    wait_bytes(got_o, out_recv.at[0])
    batch = 4

    def build_a(i, _):
        blocks = [got_o[slots[0, i * batch + j]] for j in range(batch)]
        for j in range(batch):
            t = i * batch + j
            on_left, on_right = spread(blocks[j], lanes)
            on = jnp.where(t < live[0], 1.0, 0.0)
            at = pl.multiple_of(t * BS, BS)
            a_s[pl.ds(at, BS), :] = (jnp.where(pairs[0, t] == 0, on_left, on_right) * on).astype(BF)
        return _

    lax.fori_loop(0, NT // batch, build_a, 0)
    group = 8

    def first_product(j, _):
        at = pl.multiple_of(j * 256, 256)
        weights = jnp.concatenate(
            [x_s[pl.ds(at, 128), :].astype(BF), x_s[pl.ds(at + 128, 128), :].astype(BF)], axis=1
        )
        to = pl.multiple_of(j * 128, 128)
        for g in range(NT // group):
            part = jnp.dot(
                a_s[g * group * BS:(g + 1) * group * BS, :], weights, preferred_element_type=jnp.float32
            ).astype(BF)
            for i in range(group):
                t = g * group + i
                for k in range(2):
                    h_s[pl.ds(to + k * BS, BS), t * 128:(t + 1) * 128] = part[
                        i * BS:(i + 1) * BS, k * 128:(k + 1) * 128
                    ]
        return _

    lax.fori_loop(0, 16, first_product, 0)

    wait_bytes(got_v, out_recv.at[1])

    def build_w(i, _):
        blocks = [got_v[slots[1, i * batch + j]] for j in range(batch)]
        for j in range(batch):
            t = i * batch + j
            on_left, on_right = spread(blocks[j], lanes)
            at = pl.multiple_of(t * 2 * BS, 2 * BS)
            for k in range(2):
                on = jnp.where(pairs[1, t] == k, 1.0, 0.0)
                w_s[pl.ds(at, BS), k * 128:(k + 1) * 128] = (on_left * on).astype(BF)
                w_s[pl.ds(at + BS, BS), k * 128:(k + 1) * 128] = (on_right * on).astype(BF)
        return _

    lax.fori_loop(0, NT // batch, build_w, 0)
    rows = 1024

    def second_product(j, _):
        at = pl.multiple_of(j * rows, rows)
        total = jnp.dot(h_s[pl.ds(at, rows), :], w_s[...], preferred_element_type=jnp.float32)
        for k in range(2):
            s_s[k, pl.ds(at, rows), :] = total[:, k * 128:(k + 1) * 128]
        return _

    lax.fori_loop(0, 2048 // rows, second_product, 0)

    for n in range(0, BS, 2):
        for k in range(2):
            even = s_s[k, pl.ds(n, 32, stride=BS), :]
            odd = s_s[k, pl.ds(n + 1, 32, stride=BS), :]
            at = k * BS * BS + n * BS
            t_s[0:32, at:at + 128] = jnp.where(low, even, pltpu.roll(odd, BS, 1)).astype(BF)
            t_s[32:64, at:at + 128] = jnp.where(low, pltpu.roll(even, BS, 1), odd).astype(BF)
    r_s[...] = lax.dot_general(
        t_s[...], b_ref[...], (((1,), (1,)), ((), ())), preferred_element_type=jnp.float32
    )
    for i in range(BS):
        row_s[i] = r_s[pl.ds(i, 1), :]

    def give(i, _):
        to = lax.rem(orb + i, ORBS)
        pltpu.make_async_remote_copy(
            src_ref=row_s.at[to], dst_ref=rows_got.at[orb], send_sem=row_send, recv_sem=row_recv,
            device_id=(z, to), device_id_type=MESH,
        ).start()
        return _

    lax.fori_loop(1, ORBS, give, 0)
    pltpu.make_async_copy(row_s.at[orb], rows_got.at[orb], row_recv).start()

    wait_bytes(asked.at[pl.ds(0, PEERS - 1)], req_send)
    for t in range(2):
        swaps[t].wait_send()
    for t in range(2):
        wait_bytes(own_o.at[pl.ds(0, PEERS - 1)], out_send.at[t])
        wait_bytes(other_o.at[pl.ds(0, 3 * COLS - 1)], out_send.at[t])
    for other in range(2):
        for way in range(2):
            for step in range(1, steps[way] + 1):
                hop(other, way, step).wait_send()

    wait_bytes(rows_got, row_recv)
    out[...] = jnp.sum(rows_got[...], axis=0)
    wait_bytes(rows_got.at[pl.ds(0, ORBS - 1)], row_send)


def respond(slots, pairs, live, occ, vir, requests, b):
    block = (BS // 2, 2 * BS)
    vmem = pl.BlockSpec(memory_space=pltpu.VMEM)
    smem = pl.BlockSpec(memory_space=pltpu.SMEM)
    return pl.pallas_call(
        kernel,
        out_shape=jax.ShapeDtypeStruct((1, BS), jnp.float32),
        in_specs=[smem, smem, smem, vmem, vmem, vmem, vmem],
        out_specs=vmem,
        scratch_shapes=[
            *[pltpu.VMEM((NZ, 2, GB_DEV, *block), BF)] * 2,
            *[pltpu.VMEM((PEERS, 2, *block), BF)] * 2,
            *[pltpu.VMEM((3 * COLS, 2, *block), BF)] * 2,
            *[pltpu.VMEM((ROWS // 2 * COLS * 4, *block), BF)] * 2,
            pltpu.VMEM((PEERS, 1, 128), jnp.int32),
            pltpu.SMEM((PEERS, 1, 128), jnp.int32),
            pltpu.VMEM((32 * 128, 128), jnp.float32),
            pltpu.VMEM((NT * BS, 128), BF),
            pltpu.VMEM((NT * 128, 256), BF),
            pltpu.VMEM((2048, NT * 128), BF),
            pltpu.VMEM((2, 2048, 128), jnp.float32),
            pltpu.VMEM((BS, 2 * BS * BS), BF),
            pltpu.VMEM((BS, BS), jnp.float32),
            pltpu.VMEM((ORBS, 1, BS), jnp.float32),
            pltpu.VMEM((ORBS, 1, BS), jnp.float32),
            pltpu.SemaphoreType.DMA,
            pltpu.SemaphoreType.DMA,
            pltpu.SemaphoreType.DMA((3,)),
            pltpu.SemaphoreType.DMA((2,)),
            pltpu.SemaphoreType.DMA((2,)),
            pltpu.SemaphoreType.DMA((2, 2, NZ // 2)),
            pltpu.SemaphoreType.DMA((2, 2, NZ // 2)),
            pltpu.SemaphoreType.DMA((2,)),
            pltpu.SemaphoreType.DMA((2,)),
            pltpu.SemaphoreType.DMA,
            pltpu.SemaphoreType.DMA,
        ],
        compiler_params=pltpu.CompilerParams(
            collective_id=0, has_side_effects=True, vmem_limit_bytes=56 * 2**20
        ),
        name="respond",
    )(slots, pairs, live, occ, vir, requests, b)


def local(three_centre, occ_table, vir_table, term_blocks, green_ids, live_terms):
    green = green_ids[0]
    group = green // GB_DEV
    owner = group % ORBS
    row = group // ORBS * GB_DEV + green % GB_DEV
    position = jnp.arange(NT, dtype=jnp.int32)
    earlier = position[:, None] > position[None, :]
    same = owner[:, None, :] == owner[None, :, :]
    rank = jnp.sum(jnp.logical_and(same, earlier[:, :, None]).astype(jnp.int32), axis=1)
    y, c = owner // COLS, owner % COLS
    table = jnp.arange(2, dtype=jnp.int32)[None, :]
    pair, place = (y % 4) * COLS + c, (y // 4) * 4 + table * 2 + rank
    slots = pair * 4 + (y // 4) * 2 + rank
    match = jnp.logical_and(
        pair[:, :, None, None] == jnp.arange(32, dtype=jnp.int32)[None, None, :, None],
        place[:, :, None, None] == jnp.arange(128, dtype=jnp.int32)[None, None, None, :],
    )
    requests = jnp.sum(jnp.where(match, row[:, :, None, None], 0), axis=(0, 1)).reshape(32, 1, 128)

    occ = occ_table.reshape(GB_DEV, BS, 2, 32).transpose(0, 3, 2, 1).reshape(GB_DEV, 32, 128)
    vir = vir_table.reshape(GB_DEV, 2, 32, BS).transpose(0, 2, 1, 3).reshape(GB_DEV, 32, 128)
    b = three_centre.reshape(BS, 2 * BS * BS)
    return respond(slots.T, term_blocks[0].T, live_terms.reshape(1), occ, vir, requests, b)


def solution(mesh):
    return jax.shard_map(
        local,
        mesh=mesh,
        in_specs=(
            P("aux", "orb", None),
            P(("aux", "orb"), None),
            P(("aux", "orb"), None),
            P("aux", "orb", None),
            P("aux", "orb", None),
            P("aux", "orb"),
        ),
        out_specs=P(("aux", "orb"), None),
        check_vma=False,
    )
```

```python
import functools

import jax
import jax.numpy as jnp
from jax import lax
from jax.experimental import pallas as pl
from jax.experimental.pallas import tpu as pltpu
from jax.sharding import PartitionSpec as P

BS = 64
NT = 32
GB_DEV = 4
ROWS = 8
COLS = 8
NZ = 12
REACH = 2
PEERS = (2 * REACH + 1) * COLS
ORBS = ROWS * COLS
MESH = pl.DeviceIdType.MESH
BF = jnp.bfloat16


def wait_bytes(ref, sem):
    pltpu.make_async_copy(ref, ref, sem).wait()


def spread(packed, lanes):
    wide = packed.astype(jnp.float32)
    turned = pltpu.roll(wide, BS, 1)
    zero = jnp.zeros_like(wide)
    low = lanes < BS
    left = jnp.concatenate([jnp.where(low, wide, zero), jnp.where(low, turned, zero)], axis=0)
    right = jnp.concatenate([jnp.where(low, zero, turned), jnp.where(low, zero, wide)], axis=0)
    return left, right


def kernel(
    slots, pairs, live, occ, vir, requests, b_ref, out,
    held, twin, own_o, own_v, other_o, other_v, got_o, got_v, asked, asked_s,
    b_s, x_s, a_s, w_s, h_s, s_s, t_s, r_s, row_s, rows_got,
    req_send, req_recv, copy_sem, swap_send, swap_recv, ring_send, ring_recv,
    out_send, out_recv, row_send, row_recv,
):
    z = lax.axis_index("aux")
    orb = lax.axis_index("orb")
    y, c = lax.div(orb, COLS), lax.rem(orb, COLS)
    half = lax.div(y, ROWS // 2)
    pair = lax.rem(y, ROWS // 2) * COLS + c
    right, left = lax.rem(z + 1, NZ), lax.rem(z + NZ - 1, NZ)
    opposite = lax.rem(y + ROWS // 2, ROWS) * COLS + c
    lanes = lax.broadcasted_iota(jnp.int32, (BS // 2, 2 * BS), 1)
    low = lanes < BS

    barrier = pltpu.get_barrier_semaphore()
    pl.semaphore_signal(barrier, inc=1, device_id=(right, orb), device_id_type=MESH)
    pl.semaphore_signal(barrier, inc=1, device_id=(left, orb), device_id_type=MESH)

    def greet(i, _):
        pl.semaphore_signal(barrier, inc=1, device_id=(z, lax.rem(orb + i, ORBS)), device_id_type=MESH)
        return _

    lax.fori_loop(1, ORBS, greet, 0)

    pl.semaphore_wait(barrier, ORBS + 1)

    def lay_out(k):
        for m in range(0, BS, 2):
            at = (k * BS + m) * BS
            upper = b_ref[0:32, k, m * BS:m * BS + 128].astype(jnp.float32)
            lower = b_ref[32:64, k, m * BS:m * BS + 128].astype(jnp.float32)
            b_s[0:32, at:at + 128] = upper.astype(BF)
            b_s[32:64, at:at + 128] = lower.astype(BF)
            row = k * BS + m
            x_s[pl.ds(row, 32, stride=128), :] = jnp.where(low, upper, pltpu.roll(lower, BS, 1))
            x_s[pl.ds(row + 1, 32, stride=128), :] = jnp.where(low, pltpu.roll(upper, BS, 1), lower)

    columns = (held, twin)
    outs, got = ((own_o, other_o), (own_v, other_v)), (got_o, got_v)
    own = (occ, vir)
    steps = (NZ // 2, NZ // 2 - 1)

    def hop(other, way, step):
        origin = lax.rem(z - (step - 1) + NZ, NZ) if way == 0 else lax.rem(z + step - 1, NZ)
        return pltpu.make_async_remote_copy(
            src_ref=columns[other].at[origin], dst_ref=columns[other].at[origin],
            send_sem=ring_send.at[other, way, step - 1], recv_sem=ring_recv.at[other, way, step - 1],
            device_id=(right if way == 0 else left, orb), device_id_type=MESH,
        )

    def first_hop(way):
        for t in range(2):
            pltpu.make_async_remote_copy(
                src_ref=own[t], dst_ref=held.at[z, t],
                send_sem=ring_send.at[0, way, 0], recv_sem=ring_recv.at[0, way, 0],
                device_id=(right if way == 0 else left, orb), device_id_type=MESH,
            ).start()

    def run(other, step):
        for way in range(2):
            if 1 <= step - 1 <= steps[way]:
                hop(other, way, step - 1).wait_recv()
            if step <= steps[way]:
                hop(other, way, step).start()

    def peer(e, j):
        return lax.rem(y + e + ROWS, ROWS) * COLS + lax.rem(c + j, COLS)

    def ask(e, j):
        there = lax.rem(y + e + ROWS, ROWS // 2) * COLS + lax.rem(c + j, COLS)
        pltpu.make_async_remote_copy(
            src_ref=requests.at[there], dst_ref=asked.at[(REACH - e) * COLS + c],
            send_sem=req_send, recv_sem=req_recv, device_id=(z, peer(e, j)), device_id_type=MESH,
        ).start()

    def ask_row(i, _):
        for j in range(COLS):
            ask(i - REACH + lax.div(i, REACH), j)
        return _

    def serve(t, other, e, own_row):
        box = outs[t][other]
        slot = (e + (1 if other else REACH)) * COLS
        column = (1 - half) if other else half
        for first in range(0, COLS, 4):
            some = [(j, rank) for j in range(first, first + 4) for rank in range(2)]
            rows = [
                asked_s[(e + REACH) * COLS + lax.rem(c + j, COLS), 0, column * 4 + t * 2 + rank]
                for j, rank in some
            ]
            blocks = [columns[other][lax.div(row, GB_DEV), t, lax.rem(row, GB_DEV)] for row in rows]
            for (j, rank), block in zip(some, blocks):
                box[slot + j, rank] = block
        to = got[t].at[pl.ds(pair * 4 + column * 2, 2)]
        for j in range(COLS):
            if own_row and j == 0:
                pltpu.make_async_copy(box.at[slot], to, out_recv.at[t]).start()
            else:
                pltpu.make_async_remote_copy(
                    src_ref=box.at[slot + j], dst_ref=to, send_sem=out_send.at[t], recv_sem=out_recv.at[t],
                    device_id=(z, peer(e, j)), device_id_type=MESH,
                ).start()

    def send_table(t, other):
        def one_row(i, _):
            serve(t, other, 2 * i - 1 if other else i - REACH + lax.div(i, REACH), False)
            return _

        lax.fori_loop(0, 2 if other else 2 * REACH, one_row, 0)
        serve(t, other, 0, True)

    for way in range(2):
        first_hop(way)
    swaps = [
        pltpu.make_async_remote_copy(
            src_ref=own[t], dst_ref=twin.at[z, t], send_sem=swap_send.at[t], recv_sem=swap_recv.at[t],
            device_id=(z, opposite), device_id_type=MESH,
        )
        for t in range(2)
    ]
    keeps = [pltpu.make_async_copy(own[t], held.at[z, t], copy_sem.at[t]) for t in range(2)]
    for t in range(2):
        swaps[t].start()
        keeps[t].start()
    lax.fori_loop(0, 2 * REACH, ask_row, 0)
    for j in range(1, COLS):
        ask(0, j)
    pltpu.make_async_copy(requests.at[pair], asked.at[REACH * COLS + c], req_recv).start()

    lag = 2
    last = steps[0] + 1
    to_smem = pltpu.make_async_copy(asked, asked_s, copy_sem.at[2])
    for tick in range(2, last + lag + 1):
        if tick <= last:
            run(0, tick)
        if tick == 1 + lag:
            for t in range(2):
                swaps[t].wait_recv()
        if tick > lag:
            run(1, tick - lag)
        if tick in (2, 3):
            lay_out(tick - 2)
        if tick == 5:
            wait_bytes(asked, req_recv)
            to_smem.start()
        if tick == last:
            to_smem.wait()
            for t in range(2):
                keeps[t].wait()
            send_table(0, 0)
    send_table(0, 1)
    send_table(1, 0)
    send_table(1, 1)

    wait_bytes(got_o, out_recv.at[0])
    batch = 4

    def build_a(i, _):
        blocks = [got_o[slots[0, i * batch + j]] for j in range(batch)]
        for j in range(batch):
            t = i * batch + j
            on_left, on_right = spread(blocks[j], lanes)
            on = jnp.where(t < live[0], 1.0, 0.0)
            at = pl.multiple_of(t * BS, BS)
            a_s[pl.ds(at, BS), :] = (jnp.where(pairs[0, t] == 0, on_left, on_right) * on).astype(BF)
        return _

    lax.fori_loop(0, NT // batch, build_a, 0)
    group = 8

    def first_product(j, _):
        at = pl.multiple_of(j * 256, 256)
        weights = jnp.concatenate(
            [x_s[pl.ds(at, 128), :].astype(BF), x_s[pl.ds(at + 128, 128), :].astype(BF)], axis=1
        )
        to = pl.multiple_of(j * 128, 128)
        for g in range(NT // group):
            part = jnp.dot(
                a_s[g * group * BS:(g + 1) * group * BS, :], weights, preferred_element_type=jnp.float32
            ).astype(BF)
            for i in range(group):
                t = g * group + i
                for k in range(2):
                    h_s[pl.ds(to + k * BS, BS), t * 128:(t + 1) * 128] = part[
                        i * BS:(i + 1) * BS, k * 128:(k + 1) * 128
                    ]
        return _

    lax.fori_loop(0, 16, first_product, 0)

    wait_bytes(got_v, out_recv.at[1])

    def build_w(i, _):
        blocks = [got_v[slots[1, i * batch + j]] for j in range(batch)]
        for j in range(batch):
            t = i * batch + j
            on_left, on_right = spread(blocks[j], lanes)
            at = pl.multiple_of(t * 2 * BS, 2 * BS)
            for k in range(2):
                on = jnp.where(pairs[1, t] == k, 1.0, 0.0)
                w_s[pl.ds(at, BS), k * 128:(k + 1) * 128] = (on_left * on).astype(BF)
                w_s[pl.ds(at + BS, BS), k * 128:(k + 1) * 128] = (on_right * on).astype(BF)
        return _

    lax.fori_loop(0, NT // batch, build_w, 0)
    rows = 1024

    def second_product(j, _):
        at = pl.multiple_of(j * rows, rows)
        total = jnp.dot(h_s[pl.ds(at, rows), :], w_s[...], preferred_element_type=jnp.float32)
        for k in range(2):
            s_s[k, pl.ds(at, rows), :] = total[:, k * 128:(k + 1) * 128]
        return _

    lax.fori_loop(0, 2048 // rows, second_product, 0)

    for n in range(0, BS, 2):
        for k in range(2):
            even = s_s[k, pl.ds(n, 32, stride=BS), :]
            odd = s_s[k, pl.ds(n + 1, 32, stride=BS), :]
            at = k * BS * BS + n * BS
            t_s[0:32, at:at + 128] = jnp.where(low, even, pltpu.roll(odd, BS, 1)).astype(BF)
            t_s[32:64, at:at + 128] = jnp.where(low, pltpu.roll(even, BS, 1), odd).astype(BF)
    r_s[...] = lax.dot_general(
        t_s[...], b_s[...], (((1,), (1,)), ((), ())), preferred_element_type=jnp.float32
    )
    for i in range(BS):
        row_s[i] = r_s[pl.ds(i, 1), :]

    def give(i, _):
        to = lax.rem(orb + i, ORBS)
        pltpu.make_async_remote_copy(
            src_ref=row_s.at[to], dst_ref=rows_got.at[orb], send_sem=row_send, recv_sem=row_recv,
            device_id=(z, to), device_id_type=MESH,
        ).start()
        return _

    lax.fori_loop(1, ORBS, give, 0)
    pltpu.make_async_copy(row_s.at[orb], rows_got.at[orb], row_recv).start()

    wait_bytes(asked.at[pl.ds(0, PEERS - 1)], req_send)
    for t in range(2):
        swaps[t].wait_send()
    for t in range(2):
        wait_bytes(own_o.at[pl.ds(0, PEERS - 1)], out_send.at[t])
        wait_bytes(other_o.at[pl.ds(0, 3 * COLS - 1)], out_send.at[t])
    for other in range(2):
        for way in range(2):
            for step in range(1, steps[way] + 1):
                hop(other, way, step).wait_send()

    wait_bytes(rows_got, row_recv)
    out[...] = jnp.sum(rows_got[...], axis=0)
    wait_bytes(rows_got.at[pl.ds(0, ORBS - 1)], row_send)


def respond(slots, pairs, live, occ, vir, requests, b):
    block = (BS // 2, 2 * BS)
    vmem = pl.BlockSpec(memory_space=pltpu.VMEM)
    smem = pl.BlockSpec(memory_space=pltpu.SMEM)
    return pl.pallas_call(
        kernel,
        out_shape=jax.ShapeDtypeStruct((1, BS), jnp.float32),
        in_specs=[smem, smem, smem, vmem, vmem, vmem, vmem],
        out_specs=vmem,
        scratch_shapes=[
            *[pltpu.VMEM((NZ, 2, GB_DEV, *block), BF)] * 2,
            *[pltpu.VMEM((PEERS, 2, *block), BF)] * 2,
            *[pltpu.VMEM((3 * COLS, 2, *block), BF)] * 2,
            *[pltpu.VMEM((ROWS // 2 * COLS * 4, *block), BF)] * 2,
            pltpu.VMEM((PEERS, 1, 128), jnp.int32),
            pltpu.SMEM((PEERS, 1, 128), jnp.int32),
            pltpu.VMEM((BS, 2 * BS * BS), BF),
            pltpu.VMEM((32 * 128, 128), jnp.float32),
            pltpu.VMEM((NT * BS, 128), BF),
            pltpu.VMEM((NT * 128, 256), BF),
            pltpu.VMEM((2048, NT * 128), BF),
            pltpu.VMEM((2, 2048, 128), jnp.float32),
            pltpu.VMEM((BS, 2 * BS * BS), BF),
            pltpu.VMEM((BS, BS), jnp.float32),
            pltpu.VMEM((ORBS, 1, BS), jnp.float32),
            pltpu.VMEM((ORBS, 1, BS), jnp.float32),
            pltpu.SemaphoreType.DMA,
            pltpu.SemaphoreType.DMA,
            pltpu.SemaphoreType.DMA((3,)),
            pltpu.SemaphoreType.DMA((2,)),
            pltpu.SemaphoreType.DMA((2,)),
            pltpu.SemaphoreType.DMA((2, 2, NZ // 2)),
            pltpu.SemaphoreType.DMA((2, 2, NZ // 2)),
            pltpu.SemaphoreType.DMA((2,)),
            pltpu.SemaphoreType.DMA((2,)),
            pltpu.SemaphoreType.DMA,
            pltpu.SemaphoreType.DMA,
        ],
        compiler_params=pltpu.CompilerParams(
            collective_id=0, has_side_effects=True, vmem_limit_bytes=56 * 2**20
        ),
        name="respond",
    )(slots, pairs, live, occ, vir, requests, b)


def local(three_centre, occ_table, vir_table, term_blocks, green_ids, live_terms):
    green = green_ids[0]
    group = green // GB_DEV
    owner = group % ORBS
    row = group // ORBS * GB_DEV + green % GB_DEV
    position = jnp.arange(NT, dtype=jnp.int32)
    earlier = position[:, None] > position[None, :]
    same = owner[:, None, :] == owner[None, :, :]
    rank = jnp.sum(jnp.logical_and(same, earlier[:, :, None]).astype(jnp.int32), axis=1)
    y, c = owner // COLS, owner % COLS
    table = jnp.arange(2, dtype=jnp.int32)[None, :]
    pair, place = (y % 4) * COLS + c, (y // 4) * 4 + table * 2 + rank
    slots = pair * 4 + (y // 4) * 2 + rank
    match = jnp.logical_and(
        pair[:, :, None, None] == jnp.arange(32, dtype=jnp.int32)[None, None, :, None],
        place[:, :, None, None] == jnp.arange(128, dtype=jnp.int32)[None, None, None, :],
    )
    requests = jnp.sum(jnp.where(match, row[:, :, None, None], 0), axis=(0, 1)).reshape(32, 1, 128)

    occ = occ_table.reshape(GB_DEV, BS, 2, 32).transpose(0, 3, 2, 1).reshape(GB_DEV, 32, 128)
    vir = vir_table.reshape(GB_DEV, 2, 32, BS).transpose(0, 2, 1, 3).reshape(GB_DEV, 32, 128)
    return respond(slots.T, term_blocks[0].T, live_terms.reshape(1), occ, vir, requests, three_centre)


def solution(mesh):
    return jax.shard_map(
        local,
        mesh=mesh,
        in_specs=(
            P("aux", "orb", None),
            P(("aux", "orb"), None),
            P(("aux", "orb"), None),
            P("aux", "orb", None),
            P("aux", "orb", None),
            P("aux", "orb"),
        ),
        out_specs=P(("aux", "orb"), None),
        check_vma=False,
    )
```
